512 devices in a mesh: lat: 16 (over z, x_hi), lon: 32 (over x_lo, y, core).
Axes of the slice: x: 4 (x_hi: 2, x_lo: 2; x = x_hi * 2 + x_lo), y: 8, z: 8, core: 2. Of those that a mesh axis runs over, the one named last changes fastest.
Arguments:
- fine_tokens: bfloat16 [2, 192, 384, 192], P(None, 'lat', 'lon'), may hold values from -6 to 6
- ln1_gain: float32 [192], replicated, may hold values from 0.1 to 1.9
- w_qkv1: bfloat16 [192, 576], replicated, may hold values from -6.928203 to 6.928203
- bias1: float32 [32, 1, 6, 3312], P('lat'), may hold values from -4 to 4
- w_proj1: bfloat16 [192, 192], replicated, may hold values from -0.4375 to 0.4375
- ln2_gain: float32 [192], replicated, may hold values from 0.1 to 1.9
- w_fc1: bfloat16 [192, 768], replicated, may hold values from -0.4375 to 0.4375
- w_fc2: bfloat16 [768, 192], replicated, may hold values from -0.21875 to 0.21875
- merge_gain: float32 [768], replicated, may hold values from 0.1 to 1.9
- w_merge: bfloat16 [768, 384], replicated, may hold values from -0.21875 to 0.21875
- ln3_gain: float32 [384], replicated, may hold values from 0.1 to 1.9
- w_qkv2: bfloat16 [384, 1152], replicated, may hold values from -4.8989795 to 4.8989795
- bias2: float32 [16, 1, 12, 3312], P('lat'), may hold values from -4 to 4
- w_proj2: bfloat16 [384, 384], replicated, may hold values from -0.3125 to 0.3125
Outputs:
- fine_out: bfloat16 [2, 192, 384, 192], P(None, 'lat', 'lon')
- coarse_out: bfloat16 [2, 96, 192, 384], P(None, 'lat', 'lon')
The draws below stay inside these ranges and needn't reach their ends.
All inputs are finite; a program needn't handle non-finite values.
Results may differ from the reference program's by a relative error of at most 0.039.
Values may be sent and summed in bfloat16 or wider, within the bound.
A program may use at most 128 MiB of HBM per device.

```python
import jax
import jax.numpy as jnp
import numpy as np
from jax import lax

C1 = 192
C2 = 384
HEADS1 = 6
HEADS2 = 12
FF1 = 768
WIN_Z = 2
WIN_LAT = 6
WIN_LON = 12
LEVELS = 2
LAT = 192
LON = 384
ZW = 1
LATW1 = 32
LATW2 = 16
BIAS_LEN = 3312


def drawn_qkv(key, model_width):
    query_key, other_key, value_key = jax.random.split(key, 3)
    fan_scale = model_width ** (-0.5)
    queries = jnp.clip(jax.random.normal(query_key, (model_width, model_width), jnp.float32), -4.0, 4.0) * fan_scale
    key_part = jnp.clip(jax.random.normal(other_key, (model_width, model_width), jnp.float32), -4.0, 4.0) * fan_scale
    values = jnp.clip(jax.random.normal(value_key, (model_width, model_width), jnp.float32), -4.0, 4.0) * fan_scale
    return jnp.concatenate([queries, key_part, values], axis=1).astype(jnp.bfloat16)


def draw_w_qkv1(key, part):
    key = jax.random.fold_in(key, 11)
    return drawn_qkv(key, C1)


def draw_w_qkv2(key, part):
    key = jax.random.fold_in(key, 23)
    return drawn_qkv(key, C2)


def block_levels(rng, shape, pieces, least, high):
    factor_of = 1.0
    for dim, blocks in pieces:
        steps = jax.random.uniform(jax.random.fold_in(jax.random.fold_in(rng, 6), dim), (blocks,), jnp.float32, least / len(pieces), high / len(pieces))
        factor_of = factor_of * jnp.repeat(jnp.exp(steps), shape[dim] // blocks).reshape((-1,) + (1,) * (len(shape) - 1 - dim))
    return factor_of


def bell_draw(own_key, shape, deviation, limit, cuts=(), kind=jnp.bfloat16):
    values = jax.random.normal(own_key, shape, jnp.float32) * deviation
    if len(cuts) > 0:
        values = block_levels(own_key, shape, cuts, -0.22, 0.18) * values
    return jnp.clip(values, min=-limit, max=limit).astype(kind)


def setup_inputs(seed: int = 0) -> dict:
    arg_keys = jax.random.split(jax.random.key(seed), 15)
    return {
        "fine_tokens": bell_draw(arg_keys[0], (LEVELS, LAT, LON, C1), 1.0, 6.0, ((1, 16), (2, 32))),
        "ln1_gain": jnp.clip(1.0 + 0.18 * jax.random.normal(arg_keys[1], (C1,), jnp.float32), 0.1, 1.9),
        "w_qkv1": draw_w_qkv1(jax.random.fold_in(arg_keys[14], 71), 0),
        "bias1": bell_draw(arg_keys[3], (LATW1, ZW, HEADS1, BIAS_LEN), 1.0, 4.0, ((0, 16),), jnp.float32),
        "w_proj1": bell_draw(arg_keys[4], (C1, C1), C1 ** -0.5, 0.4375),
        "ln2_gain": jnp.clip(1.0 + 0.18 * jax.random.normal(arg_keys[5], (C1,), jnp.float32), 0.1, 1.9),
        "w_fc1": bell_draw(arg_keys[6], (C1, FF1), C1 ** -0.5, 0.4375),
        "w_fc2": bell_draw(arg_keys[7], (FF1, C1), FF1 ** -0.5, 0.21875),
        "merge_gain": jnp.clip(1.0 + 0.18 * jax.random.normal(arg_keys[8], (4 * C1,), jnp.float32), 0.1, 1.9),
        "w_merge": bell_draw(arg_keys[9], (4 * C1, C2), (4 * C1) ** -0.5, 0.21875),
        "ln3_gain": jnp.clip(1.0 + 0.18 * jax.random.normal(arg_keys[10], (C2,), jnp.float32), 0.1, 1.9),
        "w_qkv2": draw_w_qkv2(jax.random.fold_in(arg_keys[14], 71), 0),
        "bias2": bell_draw(arg_keys[12], (LATW2, ZW, HEADS2, BIAS_LEN), 1.0, 4.0, ((0, 16),), jnp.float32),
        "w_proj2": bell_draw(arg_keys[13], (C2, C2), C2 ** -0.5, 0.3125),
    }


def layer_norm(inputs, scale_gain):
    average = lax.optimization_barrier(jnp.mean(inputs, axis=-1, keepdims=True))
    centred = inputs - average
    spread = lax.optimization_barrier(jnp.mean(centred * centred, axis=-1, keepdims=True))
    return centred * lax.rsqrt(spread + 1e-05) * scale_gain

def bias_index():
    tokens = np.arange(WIN_Z * WIN_LAT * WIN_LON)
    levels = tokens // (WIN_LAT * WIN_LON)
    lat_row = tokens // WIN_LON % WIN_LAT
    lon_col = tokens % WIN_LON
    flat_index = (lon_col[:, None] - lon_col[None, :] + WIN_LON - 1) * (WIN_LAT * WIN_LAT * WIN_Z * WIN_Z)
    flat_index = flat_index + (lat_row[:, None] * WIN_LAT + lat_row[None, :]) * (WIN_Z * WIN_Z)
    return (flat_index + levels[:, None] * WIN_Z + levels[None, :]).astype(np.int32)

def window_regions(level_wins, at_edge):
    tokens = jnp.arange(WIN_Z * WIN_LAT * WIN_LON, dtype=jnp.int32)
    levels = tokens // (WIN_LAT * WIN_LON)
    lat_row = tokens // WIN_LON % WIN_LAT
    last_level = (jnp.arange(level_wins, dtype=jnp.int32) == level_wins - 1)[:, None]
    upper_half = jnp.where(at_edge, (lat_row >= WIN_LAT // 2).astype(jnp.int32), 0)
    return jnp.where(last_level, levels[None, :], 0) * 2 + upper_half[None, :]

def to_windows(field_grid):
    level_count, row_count, col_count, chan_count = field_grid.shape
    split = field_grid.reshape(level_count // WIN_Z, WIN_Z, row_count // WIN_LAT, WIN_LAT, col_count // WIN_LON, WIN_LON, chan_count)
    split = split.transpose(2, 0, 4, 1, 3, 5, 6)
    return split.reshape(row_count // WIN_LAT, level_count // WIN_Z, col_count // WIN_LON, WIN_Z * WIN_LAT * WIN_LON, chan_count)

def from_windows(windows):
    row_wins, level_wins, col_wins, token_count, chan_count = windows.shape
    split = windows.reshape(row_wins, level_wins, col_wins, WIN_Z, WIN_LAT, WIN_LON, chan_count)
    split = split.transpose(1, 3, 0, 4, 2, 5, 6)
    return split.reshape(level_wins * WIN_Z, row_wins * WIN_LAT, col_wins * WIN_LON, chan_count)

def merge_patches(field_grid):
    level_count, row_count, col_count, chan_count = field_grid.shape
    paired = field_grid.reshape(level_count, row_count // 2, 2, col_count // 2, 2, chan_count)
    paired = paired.transpose(0, 1, 3, 2, 4, 5)
    return paired.reshape(level_count, row_count // 2, col_count // 2, 4 * chan_count)

def attend(windows_row, bias_rows, regions, w_qkv, w_proj, head_count):
    level_wins, col_wins, token_count, chan_count = windows_row.shape
    packed = jnp.dot(windows_row.reshape(-1, chan_count), w_qkv, preferred_element_type=jnp.float32).astype(jnp.bfloat16)
    packed = packed.reshape(level_wins, col_wins, token_count, 3, head_count, chan_count // head_count)
    queries = packed[:, :, :, 0].astype(jnp.float32)
    key_part = packed[:, :, :, 1].astype(jnp.float32)
    values = packed[:, :, :, 2].astype(jnp.float32)
    scores = jnp.einsum('zoqhd,zokhd->zohqk', queries, key_part) * (chan_count // head_count) ** (-0.5)
    bias_terms = bias_rows[:, :, bias_index()]
    scores = scores + bias_terms[:, None]
    allowed = regions[:, :, None] == regions[:, None, :]
    scores = jnp.where(allowed[:, None, None], scores, -1000000000.0)
    row_max = lax.optimization_barrier(jnp.max(scores, axis=-1, keepdims=True))
    weights = jnp.exp(scores - row_max)
    probabilities = (weights / lax.optimization_barrier(jnp.sum(weights, axis=-1, keepdims=True))).astype(jnp.bfloat16)
    blended = jnp.einsum('zohqk,zokhd->zoqhd', probabilities.astype(jnp.float32), values).astype(jnp.bfloat16)
    output = jnp.dot(blended.reshape(-1, chan_count), w_proj, preferred_element_type=jnp.float32)
    return output.reshape(level_wins, col_wins, token_count, chan_count)

def reference(fine_tokens, ln1_gain, w_qkv1, bias1, w_proj1, ln2_gain, w_fc1, w_fc2, merge_gain, w_merge, ln3_gain, w_qkv2, bias2, w_proj2):
    residual = fine_tokens.astype(jnp.float32)
    normed = layer_norm(residual, ln1_gain).astype(jnp.bfloat16)
    rolled = jnp.roll(normed, (-1, -(WIN_LAT // 2), -(WIN_LON // 2)), axis=(0, 1, 2))
    windows = to_windows(rolled)
    row_total = windows.shape[0]

    def fine_row(packed):
        windows_row, bias_rows, row_pos = packed
        regions = window_regions(windows_row.shape[0], row_pos == row_total - 1)
        return attend(windows_row, bias_rows, regions, w_qkv1, w_proj1, HEADS1)
    attention = lax.map(fine_row, (windows, bias1, jnp.arange(row_total, dtype=jnp.int32)))
    attention = jnp.roll(from_windows(attention), (1, WIN_LAT // 2, WIN_LON // 2), axis=(0, 1, 2))
    hidden = residual + attention
    normed_two = layer_norm(hidden, ln2_gain).astype(jnp.bfloat16)
    expanded = jax.nn.gelu(jnp.dot(normed_two.reshape(-1, C1), w_fc1, preferred_element_type=jnp.float32), approximate=False).astype(jnp.bfloat16)
    fine_out = (hidden + jnp.dot(expanded, w_fc2, preferred_element_type=jnp.float32).reshape(hidden.shape)).astype(jnp.bfloat16)
    merged = merge_patches(fine_out)
    merged = layer_norm(merged.astype(jnp.float32), merge_gain).astype(jnp.bfloat16)
    coarse_in = jnp.dot(merged.reshape(-1, 4 * C1), w_merge, preferred_element_type=jnp.float32).astype(jnp.bfloat16)
    coarse_in = coarse_in.reshape(merged.shape[0], merged.shape[1], merged.shape[2], C2)
    coarse_normed = layer_norm(coarse_in.astype(jnp.float32), ln3_gain).astype(jnp.bfloat16)

    def coarse_row(packed):
        windows_row, bias_rows = packed
        regions = jnp.zeros((windows_row.shape[0], WIN_Z * WIN_LAT * WIN_LON), jnp.int32)
        return attend(windows_row, bias_rows, regions, w_qkv2, w_proj2, HEADS2)
    coarse_attention = from_windows(lax.map(coarse_row, (to_windows(coarse_normed), bias2)))
    coarse_out = (coarse_in.astype(jnp.float32) + coarse_attention).astype(jnp.bfloat16)
    return (fine_out, coarse_out)
```

```python
import functools
from types import SimpleNamespace

import jax
import jax.numpy as jnp
import numpy as np
from jax import lax
from jax.experimental import pallas as pl
from jax.experimental.pallas import tpu as pltpu
from jax.sharding import PartitionSpec as P

MESH = pl.DeviceIdType.MESH
F32 = jnp.float32
BF16 = jnp.bfloat16
SCALE = 32 ** (-0.5)

SEG = dict(LC=0, LB=64, LA=176, RA=240, RB=304, RC=416, LC2=480)
SEG_ROWS = 544
TALL = dict(A=64, B=112, C=64)
SIDE = dict(A=40, B=72, C=40)
HALO = {
    "W.RA": 0, "W.RB": 64, "W.RC": 176,
    "E.LC": 240, "E.LB": 304, "E.LA": 416,
    "N.RC": 480, "N.LC": 544,
    "S.LA": 608, "S.RA": 672,
    "NW.RC": 736, "NE.LC": 800, "SW.RA": 864, "SE.LA": 928,
}
HALO_ROWS = 992
MESSAGES = (
    (0, -1, 0, 240, 240),
    (0, 1, 240, 240, 0),
    (-1, 0, 176, 128, 608),
    (1, 0, 416, 128, 480),
    (-1, -1, 176, 64, 928),
    (-1, 1, 240, 64, 864),
    (1, -1, 0, 64, 800),
    (1, 1, 416, 64, 736),
)
WINDOWS = dict(
    LB=("W.RB", "LB"),
    RB=("RB", "E.LB"),
    LC=("W.RC", "SW.RA", "LC", "S.LA"),
    RC=("RC", "S.RA", "E.LC", "SE.LA"),
    LA=("NW.RC", "W.RA", "N.LC", "LA"),
    RA=("N.RC", "RA", "NE.LC", "E.LA"),
)
SLOT = dict(LA=0, LB=256, LC=768, RA=1024, RB=1280, RC=1792)
LANES = 2048
FIRST_ROW = dict(A=0, B=3, C=9)
ROWS = dict(A=3, B=6, C=3)


def fine_row(level, row, col):
    return (row % 2 * 2 + col % 2) * 72 + col // 2 * 12 + row // 2 * 2 + level


@functools.cache
def tables():
    seg = np.zeros((SEG_ROWS, 288), np.float32)
    perm = np.zeros((288, 288), np.float32)
    for name, start in SEG.items():
        group = name[1]
        for turned in range(2):
            for col in range(6):
                for row in range(ROWS[group]):
                    place = start + (turned * 6 + col) * ROWS[group] + row
                    own_col = col + (0 if name[0] == "L" else 6)
                    source = ((FIRST_ROW[group] + row) * 12 + own_col) * 2 + 1 - turned
                    seg[place, source] = 1
                    seg[start + SIDE[group] + col * ROWS[group] + row, source] = 1
    for level in range(2):
        for row in range(12):
            for col in range(12):
                perm[fine_row(level, row, col), (row * 12 + col) * 2 + level] = 1
    spread = np.zeros((LANES, 288), np.float32)
    for name, start in SLOT.items():
        group = name[1]
        many = ROWS[group]
        for turned in range(2):
            for col in range(6):
                for head in range(6):
                    for row in range(many):
                        lane = start + turned * (128 if many == 3 else 256)
                        lane = lane + (col * 6 + head) * many + row
                        own_col = col + (0 if name[0] == "L" else 6)
                        spread[lane, fine_row(1 - turned, FIRST_ROW[group] + row, own_col)] = 1
    head_rows = np.zeros((384, 192), np.float32)
    for many, base in ((3, 0), (6, 128)):
        for lane in range(36 * many):
            head = lane // many % 6
            head_rows[base + lane, head * 32 : head * 32 + 32] = 1
    gather_a = np.zeros((216, 256), np.float32)
    gather_b = np.zeros((216, 224), np.float32)
    for level in range(2):
        for col in range(12):
            for row in range(6):
                key = level * 72 + col * 6 + row
                part = col // 6 * 2 + row // 3
                place = col % 6 * 3 + row % 3
                gather_a[key, part * 64 + level * 18 + place] = 1
                gather_a[144 + col * 6 + row, part * 64 + 40 + place] = 1
                place = col % 6 * 6 + row
                gather_b[key, col // 6 * 112 + level * 36 + place] = 1
                gather_b[144 + col * 6 + row, col // 6 * 112 + 72 + place] = 1
    pick = np.zeros((96, 256), np.float32)
    for rq in range(6):
        for level in range(2):
            for rk in range(6):
                pick[rq * 16 + level * 8 + rk, rq * 24 + rk * 4 + level * 3] = 1
    rep_b = np.zeros((184, 896), np.float32)
    rep_a = np.zeros((184, 512), np.float32)
    lane_b = np.zeros((8, 896), np.float32)
    lane_a = np.zeros((8, 512), np.float32)
    for step in range(23):
        for head in range(6):
            for row in range(6):
                lane = step * 36 + head * 6 + row
                rep_b[step * 8 + head, lane] = 1
                lane_b[row, lane] = 1
            for row in range(3):
                lane = step * 18 + head * 3 + row
                rep_a[step * 8 + head, lane] = 1
                lane_a[row, lane] = 1
    pick2 = np.zeros((192, 256), np.float32)
    for rq in range(6):
        for rk in range(6):
            for zq in range(2):
                for zk in range(2):
                    pick2[(rq * 2 + zq) * 16 + rk * 2 + zk, rq * 24 + rk * 4 + zq * 2 + zk] = 1
    rep_c = np.zeros((176, 1664), np.float32)
    lane_c = np.zeros((16, 1664), np.float32)
    for step in range(11):
        for head in range(12):
            for token in range(12):
                lane = step * 144 + head * 12 + token
                rep_c[step * 16 + head, lane] = 1
                lane_c[token, lane] = 1
    spread2 = np.zeros((896, 128), np.float32)
    head_rows2 = np.zeros((896, 384), np.float32)
    for col in range(6):
        for head in range(12):
            for token in range(12):
                lane = col * 144 + head * 12 + token
                spread2[lane, col * 12 + token] = 1
                head_rows2[lane, head * 32 : head * 32 + 32] = 1
    pad2 = np.zeros((80, 128), np.float32)
    for level in range(2):
        for row in range(6):
            for col in range(6):
                pad2[(row * 6 + col) * 2 + level, col * 12 + row * 2 + level] = 1
    return dict(
        seg=seg, perm=perm, spread=spread, head_rows=head_rows,
        pick=pick, rep_a=rep_a, lane_a=lane_a, rep_b=rep_b, lane_b=lane_b,
        pick2=pick2, rep_c=rep_c, lane_c=lane_c,
        gather_a=gather_a, gather_b=gather_b, head_cols=head_rows.T,
        collect=spread.T, unperm=perm.T, spread2=spread2, head_rows2=head_rows2,
        head_cols2=head_rows2.T, collect2=pad2 @ spread2.T, pad2=pad2,
    )


LAST = ("perm", "head_rows", "lane_b", "lane_c", "pad2")


@functools.cache
def packed():
    parts, place, row = [], {}, 0
    for name, value in tables().items():
        rows, lanes = value.shape
        tall = -(-rows // 16) * 16
        wide = -(-lanes // 128)
        padded = np.zeros((tall, wide * 128), np.float32)
        padded[:rows, :lanes] = value
        place[name] = (row, rows, tall, lanes, wide)
        for column in range(wide):
            parts.append(padded[:, column * 128 : column * 128 + 128])
        row += tall * wide
    ends = [0] + [place[name][0] + place[name][2] * place[name][4] for name in LAST]
    ranges = list(zip(ends, ends[1:]))
    return np.concatenate(parts).astype(jnp.bfloat16), place, ranges


LOADED = (
    "fine_tokens", "ln1_gain", 0, "w_qkv1", 1, 2, 3, 4, "w_proj1", "ln2_gain", "w_fc1", "w_fc2",
    "merge_gain", "w_merge", "ln3_gain", "w_qkv2", "w_proj2",
)
KEPT = tuple(name for name in LOADED if isinstance(name, str))


def mul(a, b):
    return lax.dot_general(a, b, (((1,), (0,)), ((), ())), preferred_element_type=F32)


def mul_t(a, b):
    return lax.dot_general(a, b, (((1,), (1,)), ((), ())), preferred_element_type=F32)


def norm(v, gain):
    average = jnp.mean(v, axis=-1, keepdims=True)
    centred = v - average
    spread = jnp.mean(centred * centred, axis=-1, keepdims=True)
    return centred * lax.rsqrt(spread + 1e-05) * gain


def shifted(v, start, width):
    base = start // 128 * 128
    window = -(-(start - base + width) // 128) * 128
    part = v[:, base : base + window]
    if start == base:
        return part[:, :width]
    return pltpu.roll(part, window - (start - base), 1)[:, :width]


def by_step(table, steps):
    return jnp.concatenate([by_one(table, step) for step in range(steps)], axis=0)


def by_one(table, d):
    start = d * 144
    base = start // 128 * 128
    part = table[:, base : base + 256]
    if start == base:
        return part
    return pltpu.roll(part, 256 - (start - base), 1)


def below(v, rows):
    return jnp.concatenate([v, jnp.zeros((rows - v.shape[0], v.shape[1]), F32)], axis=0).astype(BF16)


def split(v):
    high = v.astype(BF16)
    return high, (v - high.astype(F32)).astype(BF16)


def picked(pick, rows):
    return mul_t(pick, rows).astype(BF16)


def merged(parts, rep, lanes):
    wide = [mul(part, rep) for part in parts]
    total = None
    for token in range(parts[0].shape[0] // 16):
        term = sum(w[token * 16 : token * 16 + 16] for w in wide) * lanes[token : token + 1]
        total = term if total is None else total + term
    return total


def kernel(names, *refs):
    count = len(names)
    ops = SimpleNamespace(**dict(zip(names, refs[:count])))
    fine_ref, coarse_ref = refs[count : count + 2]
    rest = list(refs[count + 2 :])
    loaded = SimpleNamespace(**dict(zip(KEPT, rest[: len(KEPT)])))
    (pack, tab, tab2, own_rows, segs, halo, table_sent, table_got, table_in, table_2, queries, bias,
     bias2, mixed, rows_sent, rows_got, fine_buf, coarse_buf, load_sem, tab_sem, out_sem, send_sem,
     recv_sem) = rest[len(KEPT) :]
    _, place, ranges = packed()

    lat, lon = lax.axis_index("lat"), lax.axis_index("lon")
    lats, lons = lax.axis_size("lat"), lax.axis_size("lon")

    def at(dlat, dlon):
        return (lax.rem(lat + dlat + lats, lats), lax.rem(lon + dlon + lons, lons))

    copies = {}
    for number, name in enumerate(LOADED):
        if isinstance(name, str):
            source, target = getattr(ops, name), getattr(loaded, name)
        else:
            rows = pl.ds(ranges[name][0], ranges[name][1] - ranges[name][0])
            source, target = ops.pack.at[rows], pack.at[rows]
        copies[name] = pltpu.make_async_copy(source, target, load_sem.at[number])
    tables_in = [
        pltpu.make_async_copy(ops.bias1, table_in, tab_sem.at[0]),
        pltpu.make_async_copy(ops.bias2, table_2, tab_sem.at[1]),
    ]
    for name in LOADED[:3]:
        copies[name].start()

    barrier = pltpu.get_barrier_semaphore()
    for dlat, dlon, _, _, _ in MESSAGES:
        pl.semaphore_signal(barrier, inc=1, device_id=at(dlat, dlon), device_id_type=MESH)
    for copy in tables_in:
        copy.start()
    for name in LOADED[3:]:
        copies[name].start()

    def arrived(name):
        copies[name].wait()
        return getattr(loaded, name)

    get = SimpleNamespace(**{name: functools.partial(arrived, name) for name in KEPT})

    def table(name):
        first, rows, tall, lanes, wide = place[name]
        parts = [pack[first + tall * c : first + tall * c + rows, :] for c in range(wide)]
        value = parts[0] if wide == 1 else jnp.concatenate(parts, axis=1)
        return value[:, :lanes]

    const = SimpleNamespace(**{name: functools.partial(table, name) for name in place})

    gain1 = get.ln1_gain()[...]
    own_tokens = get.fine_tokens()
    for token in range(144):
        own_rows[token * 2 : token * 2 + 2, :] = own_tokens[token].astype(F32)
    raw = own_rows[...]
    normed = norm(raw, gain1)
    level = lax.broadcasted_iota(jnp.int32, (288, 1), 0) % 2
    side = jnp.concatenate([normed[:, 128:], jnp.zeros((288, 64), F32)], axis=1)
    side = jnp.where(level == 1, side, pltpu.roll(side, 64, 1))
    normed = normed.astype(BF16)
    copies[0].wait()
    cut = mul(const.seg(), jnp.concatenate([normed[:, :128], side.astype(BF16)], axis=1))
    pieces = []
    for name, first in SEG.items():
        middle, end = first + SIDE[name[1]], first + TALL[name[1]]
        pieces += [cut[first:middle, :128], cut[middle:end, 128:]]
    segs[...] = jnp.concatenate(pieces, axis=0).astype(BF16)

    pl.semaphore_wait(barrier, len(MESSAGES))
    sends = []
    for number, (dlat, dlon, first, many, there) in enumerate(MESSAGES):
        sends.append(
            pltpu.make_async_remote_copy(
                src_ref=segs.at[pl.ds(first, many)], dst_ref=halo.at[pl.ds(there, many)],
                send_sem=send_sem.at[number], recv_sem=recv_sem.at[number],
                device_id=at(dlat, dlon), device_id_type=MESH,
            )
        )
    for number in (2, 3, 4, 5, 6, 7, 0, 1):
        sends[number].start()

    tables_in[0].wait()
    copies[2].wait()
    tab[...] = jnp.zeros_like(tab)
    pick = const.pick()

    def steps_of(first_head):
        for head in range(6):
            tab[head : head + 1, :3312] = table_in[first_head + head]
        return split(by_step(tab[...], 23))

    high, low = steps_of(6)
    high = picked(pick, high)
    table_sent[...] = high[48:]
    table_copy = pltpu.make_async_remote_copy(
        src_ref=table_sent, dst_ref=table_got, send_sem=send_sem.at[8], recv_sem=recv_sem.at[8],
        device_id=at(1, 0), device_id_type=MESH,
    )
    table_copy.start()
    parts_c = (high[:48], picked(pick[:48], low))
    high, low = steps_of(0)
    parts_b = (picked(pick, high), picked(pick, low))
    rep_a, lane_a = const.rep_a(), const.lane_a().astype(F32)
    key_row = lax.broadcasted_iota(jnp.int32, (16, 1), 0) % 8

    def lay_bias(group, value):
        per_col = 6 * ROWS[group]
        wide = 128 if group != "B" else 256
        for half in "LR":
            start = SLOT[half + group]
            for key_col in range(12):
                first = ((17 if half == "L" else 11) - key_col) * per_col
                part = shifted(value, first, wide)
                for level in range(2):
                    lo = start + level * wide
                    bias[key_col * 6 : key_col * 6 + 6, lo : lo + wide] = part[level * 8 : level * 8 + 6]

    lay_bias("B", merged(parts_b, const.rep_b(), const.lane_b().astype(F32)))
    value = merged(parts_c, rep_a, lane_a)
    lay_bias("C", jnp.where(jnp.logical_and(key_row >= 3, lat == lats - 1), -1e9, value))

    own = mul(const.perm(), raw.astype(BF16))
    own_normed = mul(const.perm(), normed).astype(BF16)
    w_qkv1 = get.w_qkv1()[...]
    own_queries = mul(own_normed, w_qkv1[:, :192]).astype(BF16)
    w_key = pltpu.roll(w_qkv1[:, 128:384].astype(F32), 192, 1)[:, :192].astype(BF16)
    w_value = w_qkv1[:, 384:]

    def unit(size):
        rows = lax.broadcasted_iota(jnp.int32, (size, size), 0)
        cols = lax.broadcasted_iota(jnp.int32, (size, size), 1)
        return jnp.where(rows == cols, 1.0, 0.0).astype(BF16)

    def placed(w, level):
        zeros = jnp.zeros((64, w.shape[1]), BF16)
        tail = (w[128:], zeros) if level == 0 else (zeros, w[128:])
        return jnp.concatenate((w[:128],) + tail, axis=0)

    w_keys = [placed(w_key, level) for level in range(2)]
    w_values_t = [mul_t(unit(192), placed(w_value, level)).astype(BF16) for level in range(2)]
    copies[1].wait()
    spread = const.spread()
    head_rows = const.head_rows().astype(F32)
    for name, start in SLOT.items():
        wide = 128 if name[1] != "B" else 256
        mask = head_rows[:128] if name[1] != "B" else head_rows[128:]
        for level in range(2):
            lo = start + level * wide
            queries[lo : lo + wide, :] = (mul(spread[lo : lo + wide], own_queries) * mask).astype(BF16)

    copies[4].wait()
    gathers = dict(A=const.gather_a(), B=const.gather_b())
    gathers.update(C=gathers["A"])
    head_cols = const.head_cols().astype(F32)

    def attend(name):
        group = name[1]
        pieces = []
        for part in WINDOWS[name]:
            source, first = (halo, HALO[part]) if part in HALO else (segs, SEG[part])
            pieces.append(source[first : first + TALL[group], :])
        tokens = mul(gathers[group], jnp.concatenate(pieces, axis=0))
        wide = 128 if group != "B" else 256
        mask = head_cols[:, :128] if group != "B" else head_cols[:, 128:]
        for level in range(2):
            lo = SLOT[name] + level * wide
            level_tokens = jnp.concatenate([tokens[level * 72 : level * 72 + 72], tokens[144:]], axis=1)
            level_tokens = level_tokens.astype(BF16)
            keys = mul(level_tokens, w_keys[level]).astype(BF16)
            values_t = mul_t(w_values_t[level], level_tokens).astype(BF16)
            scores = mul_t(keys, queries[lo : lo + wide, :]) * SCALE + bias[:, lo : lo + wide]
            weights = jnp.exp(scores - jnp.max(scores, axis=0, keepdims=True))
            probs = weights * (1.0 / jnp.sum(weights, axis=0, keepdims=True))
            mixed[:, lo : lo + wide] = (mul(values_t, probs.astype(BF16)) * mask).astype(BF16)

    tables_in[1].wait()
    tab2[...] = jnp.zeros_like(tab2)
    for head in range(12):
        tab2[head : head + 1, :3312] = table_2[head]
    on_left = lon % 2 == 0
    rows2 = by_step(tab2[...], 23)
    copies[3].wait()
    pick2, rep_c, lane_c = const.pick2(), const.rep_c(), const.lane_c().astype(F32)
    for part in range(2):
        steps = rows2[96:272] if part == 0 else jnp.where(on_left, rows2[:176], rows2[192:])
        high, low = split(steps)
        value = merged((picked(pick2, high), picked(pick2, low)), rep_c, lane_c)
        for key_col in range(6):
            first = part * 72 + key_col * 12
            bias2[first : first + 12, :] = shifted(value, (5 - key_col) * 144, 896)[:12]

    sends[0].wait()
    sends[1].wait()
    attend("LB")
    attend("RB")
    table_copy.wait()
    value = merged((table_got[...],), rep_a, lane_a)
    lay_bias("A", jnp.where(jnp.logical_and(key_row < 3, lat == 0), -1e9, value))
    for send in sends[2:]:
        send.wait()
    for name in ("LC", "RC", "LA", "RA"):
        attend(name)

    heads = mul_t(const.collect(), mixed[...]).astype(BF16)
    hidden = own + mul(heads, get.w_proj1()[...])
    normed2 = norm(hidden, get.ln2_gain()[...]).astype(BF16)
    inner = mul(normed2, get.w_fc1()[...])
    expanded = (0.5 * inner * (1.0 + lax.erf(inner * (0.5**0.5)))).astype(BF16)
    fine = (hidden + mul_t(expanded, get.w_fc2()[...])).astype(BF16)
    fine_rows = mul(const.unperm(), fine)
    for token in range(144):
        fine_buf[token] = fine_rows[token * 2 : token * 2 + 2].astype(BF16)
    fine_out = pltpu.make_async_copy(fine_buf, fine_ref, out_sem.at[0])
    fine_out.start()

    fine = fine.astype(F32)
    patches = [fine[p * 72 : p * 72 + 72] for p in range(4)]
    total = sum(jnp.sum(p, axis=-1, keepdims=True) for p in patches)
    centred = [p - total * (1.0 / 768) for p in patches]
    total = sum(jnp.sum(p * p, axis=-1, keepdims=True) for p in centred)
    factor = lax.rsqrt(total * (1.0 / 768) + 1e-05)
    gain = get.merge_gain()[...]
    gain = jnp.concatenate([gain[i : i + 1] for i in range(6)], axis=1)
    gain = jnp.broadcast_to(gain, (8, 768))
    w_merge = get.w_merge()[...]
    coarse = None
    for p in range(4):
        part_gain = shifted(gain, p * 192, 192)[:1]
        part = (centred[p] * factor * part_gain).astype(BF16)
        term = mul(part, w_merge[p * 192 : p * 192 + 192])
        coarse = term if coarse is None else coarse + term
    coarse = coarse.astype(BF16)
    gain = get.ln3_gain()[...]
    gain = jnp.concatenate([gain[i : i + 1] for i in range(3)], axis=1)
    normed3 = norm(coarse.astype(F32), gain)
    rows_sent[...] = below(normed3, 80)
    partner = (lat, lon + 1 - 2 * lax.rem(lon, 2))
    swap = pltpu.make_async_remote_copy(
        src_ref=rows_sent, dst_ref=rows_got, send_sem=send_sem.at[9], recv_sem=recv_sem.at[9],
        device_id=partner, device_id_type=MESH,
    )
    swap.start()

    normed3 = normed3.astype(BF16)
    w_qkv2 = get.w_qkv2()
    w_key2 = w_qkv2[:, 384:768]
    w_value2_t = mul_t(unit(384), w_qkv2[:, 768:]).astype(BF16)
    own_queries2 = below(mul(normed3, w_qkv2[:, :384]), 128)
    queries2 = (mul(const.spread2(), own_queries2) * const.head_rows2().astype(F32)).astype(BF16)
    coarse_pad = mul(const.pad2(), below(coarse.astype(F32), 128))
    head_cols2, collect2, w_proj2 = const.head_cols2().astype(F32), const.collect2(), get.w_proj2()[...]

    def scored(tokens, part):
        keys = mul(tokens, w_key2).astype(BF16)
        return mul_t(keys, queries2) * SCALE + bias2[part * 72 : part * 72 + 72, :]

    scores_near = scored(normed3, 0)
    values_near = mul_t(w_value2_t, normed3).astype(BF16)
    swap.wait()
    other = rows_got[...].astype(F32)[:72].astype(BF16)
    scores_far = scored(other, 1)
    values_far = mul_t(w_value2_t, other).astype(BF16)
    top = jnp.maximum(
        jnp.max(scores_near, axis=0, keepdims=True), jnp.max(scores_far, axis=0, keepdims=True)
    )
    near = jnp.exp(scores_near - top)
    far = jnp.exp(scores_far - top)
    factor = 1.0 / (jnp.sum(near, axis=0, keepdims=True) + jnp.sum(far, axis=0, keepdims=True))
    blended = mul(values_near, (near * factor).astype(BF16)) + mul(values_far, (far * factor).astype(BF16))
    heads2 = mul_t(collect2, (blended * head_cols2).astype(BF16)).astype(BF16)
    result = coarse_pad + mul(heads2, w_proj2)
    for token in range(36):
        coarse_buf[token] = result[token * 2 : token * 2 + 2].astype(BF16)
    coarse_out = pltpu.make_async_copy(coarse_buf, coarse_ref, out_sem.at[1])
    coarse_out.start()
    fine_out.wait()
    coarse_out.wait()


def shards(
    fine_tokens, ln1_gain, w_qkv1, bias1, w_proj1, ln2_gain, w_fc1, w_fc2, merge_gain, w_merge,
    ln3_gain, w_qkv2, bias2, w_proj2,
):
    ops = dict(
        fine_tokens=fine_tokens.transpose(1, 2, 0, 3).reshape(144, 2, 192),
        ln1_gain=ln1_gain.reshape(1, 192), w_qkv1=w_qkv1, bias1=bias1.reshape(12, 1, 3312),
        w_proj1=w_proj1, ln2_gain=ln2_gain.reshape(1, 192), w_fc1=w_fc1, w_fc2=w_fc2.T,
        merge_gain=merge_gain.reshape(6, 128), w_merge=w_merge, ln3_gain=ln3_gain.reshape(3, 128),
        w_qkv2=w_qkv2, bias2=bias2.reshape(12, 1, 3312), w_proj2=w_proj2,
        pack=jnp.asarray(packed()[0]),
    )
    names = tuple(ops)
    any_space = pl.BlockSpec(memory_space=pl.ANY)
    scratch = [pltpu.VMEM(ops[name].shape, ops[name].dtype) for name in KEPT]
    scratch += [
        pltpu.VMEM(packed()[0].shape, BF16),
        pltpu.VMEM((8, 3328), F32),
        pltpu.VMEM((16, 3328), F32),
        pltpu.VMEM((288, 192), F32),
        pltpu.VMEM((SEG_ROWS, 128), BF16),
        pltpu.VMEM((HALO_ROWS, 128), BF16),
        pltpu.VMEM((48, 184), BF16),
        pltpu.VMEM((48, 184), BF16),
        pltpu.VMEM((12, 1, 3312), F32),
        pltpu.VMEM((12, 1, 3312), F32),
        pltpu.VMEM((LANES, 192), BF16),
        pltpu.VMEM((72, LANES), F32),
        pltpu.VMEM((144, 896), F32),
        pltpu.VMEM((192, LANES), BF16),
        pltpu.VMEM((80, 384), BF16),
        pltpu.VMEM((80, 384), BF16),
        pltpu.VMEM((144, 2, 192), BF16),
        pltpu.VMEM((36, 2, 384), BF16),
        pltpu.SemaphoreType.DMA((len(LOADED),)),
        pltpu.SemaphoreType.DMA((2,)),
        pltpu.SemaphoreType.DMA((2,)),
        pltpu.SemaphoreType.DMA((10,)),
        pltpu.SemaphoreType.DMA((10,)),
    ]
    fine, coarse = pl.pallas_call(
        functools.partial(kernel, names),
        out_shape=(
            pltpu.VMEM((144, 2, 192), BF16),
            pltpu.VMEM((36, 2, 384), BF16),
        ),
        in_specs=[pl.BlockSpec(memory_space=pl.ANY)] * len(names),
        out_specs=(any_space, any_space),
        scratch_shapes=scratch,
        compiler_params=pltpu.CompilerParams(
            collective_id=0, has_side_effects=True, vmem_limit_bytes=56 * 1024 * 1024
        ),
        cost_estimate=pl.CostEstimate(
            flops=2_000_000_000, bytes_accessed=12_000_000, transcendentals=1_000_000
        ),
    )(*ops.values())
    fine = fine.reshape(12, 12, 2, 192).transpose(2, 0, 1, 3)
    return fine, coarse.reshape(6, 6, 2, 384).transpose(2, 0, 1, 3)


def solution(mesh):
    whole, by_lat, grid = P(), P("lat", None, None, None), P(None, "lat", "lon", None)
    in_specs = (grid, whole, whole, by_lat) + (whole,) * 8 + (by_lat, whole)
    return jax.shard_map(
        shards, mesh=mesh, in_specs=in_specs, out_specs=(grid, grid), check_vma=False
    )
```

```python
import functools
from types import SimpleNamespace

import jax
import jax.numpy as jnp
import numpy as np
from jax import lax
from jax.experimental import pallas as pl
from jax.experimental.pallas import tpu as pltpu
from jax.sharding import PartitionSpec as P

MESH = pl.DeviceIdType.MESH
F32 = jnp.float32
BF16 = jnp.bfloat16
SCALE = 32 ** (-0.5)

SEG = dict(LC=0, LB=64, LA=176, RA=240, RB=304, RC=416, LC2=480)
SEG_ROWS = 544
TALL = dict(A=64, B=112, C=64)
SIDE = dict(A=40, B=72, C=40)
HALO = {
    "W.RA": 0, "W.RB": 64, "W.RC": 176,
    "E.LC": 240, "E.LB": 304, "E.LA": 416,
    "N.RC": 480, "N.LC": 544,
    "S.LA": 608, "S.RA": 672,
    "NW.RC": 736, "NE.LC": 800, "SW.RA": 864, "SE.LA": 928,
}
HALO_ROWS = 992
MESSAGES = (
    (0, -1, 0, 240, 240),
    (0, 1, 240, 240, 0),
    (-1, 0, 176, 128, 608),
    (1, 0, 416, 128, 480),
    (-1, -1, 176, 64, 928),
    (-1, 1, 240, 64, 864),
    (1, -1, 0, 64, 800),
    (1, 1, 416, 64, 736),
)
WINDOWS = dict(
    LB=("W.RB", "LB"),
    RB=("RB", "E.LB"),
    LC=("W.RC", "SW.RA", "LC", "S.LA"),
    RC=("RC", "S.RA", "E.LC", "SE.LA"),
    LA=("NW.RC", "W.RA", "N.LC", "LA"),
    RA=("N.RC", "RA", "NE.LC", "E.LA"),
)
SLOT = dict(LA=0, LB=256, LC=768, RA=1024, RB=1280, RC=1792)
LANES = 2048
FIRST_ROW = dict(A=0, B=3, C=9)
ROWS = dict(A=3, B=6, C=3)


def fine_row(level, row, col):
    return (row % 2 * 2 + col % 2) * 72 + col // 2 * 12 + row // 2 * 2 + level


@functools.cache
def tables():
    seg = np.zeros((SEG_ROWS, 288), np.float32)
    perm = np.zeros((288, 288), np.float32)
    for name, start in SEG.items():
        group = name[1]
        for turned in range(2):
            for col in range(6):
                for row in range(ROWS[group]):
                    place = start + (turned * 6 + col) * ROWS[group] + row
                    own_col = col + (0 if name[0] == "L" else 6)
                    source = ((FIRST_ROW[group] + row) * 12 + own_col) * 2 + 1 - turned
                    seg[place, source] = 1
                    seg[start + SIDE[group] + col * ROWS[group] + row, source] = 1
    for level in range(2):
        for row in range(12):
            for col in range(12):
                perm[fine_row(level, row, col), (row * 12 + col) * 2 + level] = 1
    spread = np.zeros((LANES, 288), np.float32)
    for name, start in SLOT.items():
        group = name[1]
        many = ROWS[group]
        for turned in range(2):
            for col in range(6):
                for head in range(6):
                    for row in range(many):
                        lane = start + turned * (128 if many == 3 else 256)
                        lane = lane + (col * 6 + head) * many + row
                        own_col = col + (0 if name[0] == "L" else 6)
                        spread[lane, fine_row(1 - turned, FIRST_ROW[group] + row, own_col)] = 1
    head_rows = np.zeros((384, 192), np.float32)
    for many, base in ((3, 0), (6, 128)):
        for lane in range(36 * many):
            head = lane // many % 6
            head_rows[base + lane, head * 32 : head * 32 + 32] = 1
    gather_a = np.zeros((216, 256), np.float32)
    gather_b = np.zeros((216, 224), np.float32)
    for level in range(2):
        for col in range(12):
            for row in range(6):
                key = level * 72 + col * 6 + row
                part = col // 6 * 2 + row // 3
                place = col % 6 * 3 + row % 3
                gather_a[key, part * 64 + level * 18 + place] = 1
                gather_a[144 + col * 6 + row, part * 64 + 40 + place] = 1
                place = col % 6 * 6 + row
                gather_b[key, col // 6 * 112 + level * 36 + place] = 1
                gather_b[144 + col * 6 + row, col // 6 * 112 + 72 + place] = 1
    pick = np.zeros((96, 256), np.float32)
    for rq in range(6):
        for level in range(2):
            for rk in range(6):
                pick[rq * 16 + level * 8 + rk, rq * 24 + rk * 4 + level * 3] = 1
    rep_b = np.zeros((184, 896), np.float32)
    rep_a = np.zeros((184, 512), np.float32)
    lane_b = np.zeros((8, 896), np.float32)
    lane_a = np.zeros((8, 512), np.float32)
    for step in range(23):
        for head in range(6):
            for row in range(6):
                lane = step * 36 + head * 6 + row
                rep_b[step * 8 + head, lane] = 1
                lane_b[row, lane] = 1
            for row in range(3):
                lane = step * 18 + head * 3 + row
                rep_a[step * 8 + head, lane] = 1
                lane_a[row, lane] = 1
    pick2 = np.zeros((192, 256), np.float32)
    for rq in range(6):
        for rk in range(6):
            for zq in range(2):
                for zk in range(2):
                    pick2[(rq * 2 + zq) * 16 + rk * 2 + zk, rq * 24 + rk * 4 + zq * 2 + zk] = 1
    rep_c = np.zeros((176, 1664), np.float32)
    lane_c = np.zeros((16, 1664), np.float32)
    for step in range(11):
        for head in range(12):
            for token in range(12):
                lane = step * 144 + head * 12 + token
                rep_c[step * 16 + head, lane] = 1
                lane_c[token, lane] = 1
    spread2 = np.zeros((896, 128), np.float32)
    head_rows2 = np.zeros((896, 384), np.float32)
    for col in range(6):
        for head in range(12):
            for token in range(12):
                lane = col * 144 + head * 12 + token
                spread2[lane, col * 12 + token] = 1
                head_rows2[lane, head * 32 : head * 32 + 32] = 1
    pad2 = np.zeros((80, 128), np.float32)
    for level in range(2):
        for row in range(6):
            for col in range(6):
                pad2[(row * 6 + col) * 2 + level, col * 12 + row * 2 + level] = 1
    return dict(
        seg=seg, perm=perm, spread=spread, head_rows=head_rows,
        pick=pick, rep_a=rep_a, lane_a=lane_a, rep_b=rep_b, lane_b=lane_b,
        pick2=pick2, rep_c=rep_c, lane_c=lane_c,
        gather_a=gather_a, gather_b=gather_b, head_cols=head_rows.T,
        collect=spread.T, unperm=perm.T, spread2=spread2, head_rows2=head_rows2,
        head_cols2=head_rows2.T, collect2=pad2 @ spread2.T, pad2=pad2,
    )


LAST = ("perm", "head_rows", "lane_b", "lane_c", "pad2")


@functools.cache
def packed():
    parts, place, row = [], {}, 0
    for name, value in tables().items():
        rows, lanes = value.shape
        tall = -(-rows // 16) * 16
        wide = -(-lanes // 128)
        padded = np.zeros((tall, wide * 128), np.float32)
        padded[:rows, :lanes] = value
        place[name] = (row, rows, tall, lanes, wide)
        for column in range(wide):
            parts.append(padded[:, column * 128 : column * 128 + 128])
        row += tall * wide
    ends = [0] + [place[name][0] + place[name][2] * place[name][4] for name in LAST]
    ranges = list(zip(ends, ends[1:]))
    return np.concatenate(parts).astype(jnp.bfloat16), place, ranges


LOADED = (
    "fine_tokens", "ln1_gain", 0, "w_qkv1", 1, 2, 3, 4, "w_proj1", "ln2_gain", "w_fc1", "w_fc2",
    "merge_gain", "w_merge", "ln3_gain", "w_qkv2", "w_proj2",
)
KEPT = tuple(name for name in LOADED if isinstance(name, str))


def mul(a, b):
    return lax.dot_general(a, b, (((1,), (0,)), ((), ())), preferred_element_type=F32)


def mul_t(a, b):
    return lax.dot_general(a, b, (((1,), (1,)), ((), ())), preferred_element_type=F32)


def norm(v, gain):
    average = jnp.mean(v, axis=-1, keepdims=True)
    centred = v - average
    spread = jnp.mean(centred * centred, axis=-1, keepdims=True)
    return centred * lax.rsqrt(spread + 1e-05) * gain


def shifted(v, start, width):
    base = start // 128 * 128
    window = -(-(start - base + width) // 128) * 128
    part = v[:, base : base + window]
    if start == base:
        return part[:, :width]
    return pltpu.roll(part, window - (start - base), 1)[:, :width]


def by_step(table, steps):
    return jnp.concatenate([by_one(table, step) for step in range(steps)], axis=0)


def by_one(table, d):
    start = d * 144
    base = start // 128 * 128
    part = table[:, base : base + 256]
    if start == base:
        return part
    return pltpu.roll(part, 256 - (start - base), 1)


def below(v, rows):
    return jnp.concatenate([v, jnp.zeros((rows - v.shape[0], v.shape[1]), F32)], axis=0).astype(BF16)


def split(v):
    high = v.astype(BF16)
    return high, (v - high.astype(F32)).astype(BF16)


def picked(pick, rows):
    return mul_t(pick, rows).astype(BF16)


def merged(parts, rep, lanes):
    wide = [mul(part, rep) for part in parts]
    total = None
    for token in range(parts[0].shape[0] // 16):
        term = sum(w[token * 16 : token * 16 + 16] for w in wide) * lanes[token : token + 1]
        total = term if total is None else total + term
    return total


def kernel(names, *refs):
    count = len(names)
    ops = SimpleNamespace(**dict(zip(names, refs[:count])))
    fine_ref, coarse_ref = refs[count : count + 2]
    rest = list(refs[count + 2 :])
    loaded = SimpleNamespace(**dict(zip(KEPT, rest[: len(KEPT)])))
    (pack, tab, tab2, own_rows, segs, halo, table_sent, table_got, table_in, table_2, queries, bias,
     bias2, mixed, rows_sent, rows_got, load_sem, tab_sem, send_sem,
     recv_sem) = rest[len(KEPT) :]
    _, place, ranges = packed()

    lat, lon = lax.axis_index("lat"), lax.axis_index("lon")
    lats, lons = lax.axis_size("lat"), lax.axis_size("lon")

    def at(dlat, dlon):
        return (lax.rem(lat + dlat + lats, lats), lax.rem(lon + dlon + lons, lons))

    copies = {}
    for number, name in enumerate(LOADED):
        if isinstance(name, str):
            source, target = getattr(ops, name), getattr(loaded, name)
        else:
            rows = pl.ds(ranges[name][0], ranges[name][1] - ranges[name][0])
            source, target = ops.pack.at[rows], pack.at[rows]
        copies[name] = pltpu.make_async_copy(source, target, load_sem.at[number])
    tables_in = [
        pltpu.make_async_copy(ops.bias1, table_in, tab_sem.at[0]),
        pltpu.make_async_copy(ops.bias2, table_2, tab_sem.at[1]),
    ]
    for name in LOADED[:3]:
        copies[name].start()

    barrier = pltpu.get_barrier_semaphore()
    for dlat, dlon, _, _, _ in MESSAGES:
        pl.semaphore_signal(barrier, inc=1, device_id=at(dlat, dlon), device_id_type=MESH)
    for copy in tables_in:
        copy.start()
    for name in LOADED[3:]:
        copies[name].start()

    def arrived(name):
        copies[name].wait()
        return getattr(loaded, name)

    get = SimpleNamespace(**{name: functools.partial(arrived, name) for name in KEPT})

    def table(name):
        first, rows, tall, lanes, wide = place[name]
        parts = [pack[first + tall * c : first + tall * c + rows, :] for c in range(wide)]
        value = parts[0] if wide == 1 else jnp.concatenate(parts, axis=1)
        return value[:, :lanes]

    const = SimpleNamespace(**{name: functools.partial(table, name) for name in place})

    gain1 = get.ln1_gain()[...]
    own_tokens = get.fine_tokens()
    for token in range(144):
        own_rows[token * 2 : token * 2 + 2, :] = own_tokens[token].astype(F32)
    raw = own_rows[...]
    normed = norm(raw, gain1)
    level = lax.broadcasted_iota(jnp.int32, (288, 1), 0) % 2
    side = jnp.concatenate([normed[:, 128:], jnp.zeros((288, 64), F32)], axis=1)
    side = jnp.where(level == 1, side, pltpu.roll(side, 64, 1))
    normed = normed.astype(BF16)
    copies[0].wait()
    cut = mul(const.seg(), jnp.concatenate([normed[:, :128], side.astype(BF16)], axis=1))
    pieces = []
    for name, first in SEG.items():
        middle, end = first + SIDE[name[1]], first + TALL[name[1]]
        pieces += [cut[first:middle, :128], cut[middle:end, 128:]]
    segs[...] = jnp.concatenate(pieces, axis=0).astype(BF16)

    pl.semaphore_wait(barrier, len(MESSAGES))
    sends = []
    for number, (dlat, dlon, first, many, there) in enumerate(MESSAGES):
        sends.append(
            pltpu.make_async_remote_copy(
                src_ref=segs.at[pl.ds(first, many)], dst_ref=halo.at[pl.ds(there, many)],
                send_sem=send_sem.at[number], recv_sem=recv_sem.at[number],
                device_id=at(dlat, dlon), device_id_type=MESH,
            )
        )
    for number in (2, 3, 4, 5, 6, 7, 0, 1):
        sends[number].start()

    tables_in[0].wait()
    copies[2].wait()
    tab[...] = jnp.zeros_like(tab)
    pick = const.pick()

    def steps_of(first_head):
        for head in range(6):
            tab[head : head + 1, :3312] = table_in[first_head + head]
        return split(by_step(tab[...], 23))

    high, low = steps_of(6)
    high = picked(pick, high)
    table_sent[...] = high[48:]
    table_copy = pltpu.make_async_remote_copy(
        src_ref=table_sent, dst_ref=table_got, send_sem=send_sem.at[8], recv_sem=recv_sem.at[8],
        device_id=at(1, 0), device_id_type=MESH,
    )
    table_copy.start()
    parts_c = (high[:48], picked(pick[:48], low))
    high, low = steps_of(0)
    parts_b = (picked(pick, high), picked(pick, low))
    rep_a, lane_a = const.rep_a(), const.lane_a().astype(F32)
    key_row = lax.broadcasted_iota(jnp.int32, (16, 1), 0) % 8

    def lay_bias(group, value):
        per_col = 6 * ROWS[group]
        wide = 128 if group != "B" else 256
        for half in "LR":
            start = SLOT[half + group]
            for key_col in range(12):
                first = ((17 if half == "L" else 11) - key_col) * per_col
                part = shifted(value, first, wide)
                for level in range(2):
                    lo = start + level * wide
                    bias[key_col * 6 : key_col * 6 + 6, lo : lo + wide] = part[level * 8 : level * 8 + 6]

    lay_bias("B", merged(parts_b, const.rep_b(), const.lane_b().astype(F32)))
    value = merged(parts_c, rep_a, lane_a)
    lay_bias("C", jnp.where(jnp.logical_and(key_row >= 3, lat == lats - 1), -1e9, value))

    own = mul(const.perm(), raw.astype(BF16))
    own_normed = mul(const.perm(), normed).astype(BF16)
    w_qkv1 = get.w_qkv1()[...]
    own_queries = mul(own_normed, w_qkv1[:, :192]).astype(BF16)
    w_key = pltpu.roll(w_qkv1[:, 128:384].astype(F32), 192, 1)[:, :192].astype(BF16)
    w_value = w_qkv1[:, 384:]

    def unit(size):
        rows = lax.broadcasted_iota(jnp.int32, (size, size), 0)
        cols = lax.broadcasted_iota(jnp.int32, (size, size), 1)
        return jnp.where(rows == cols, 1.0, 0.0).astype(BF16)

    def placed(w, level):
        zeros = jnp.zeros((64, w.shape[1]), BF16)
        tail = (w[128:], zeros) if level == 0 else (zeros, w[128:])
        return jnp.concatenate((w[:128],) + tail, axis=0)

    w_keys = [placed(w_key, level) for level in range(2)]
    w_values_t = [mul_t(unit(192), placed(w_value, level)).astype(BF16) for level in range(2)]
    copies[1].wait()
    spread = const.spread()
    head_rows = const.head_rows().astype(F32)
    for name, start in SLOT.items():
        wide = 128 if name[1] != "B" else 256
        mask = head_rows[:128] if name[1] != "B" else head_rows[128:]
        for level in range(2):
            lo = start + level * wide
            queries[lo : lo + wide, :] = (mul(spread[lo : lo + wide], own_queries) * mask).astype(BF16)

    copies[4].wait()
    gathers = dict(A=const.gather_a(), B=const.gather_b())
    gathers.update(C=gathers["A"])
    head_cols = const.head_cols().astype(F32)

    def attend(name):
        group = name[1]
        pieces = []
        for part in WINDOWS[name]:
            source, first = (halo, HALO[part]) if part in HALO else (segs, SEG[part])
            pieces.append(source[first : first + TALL[group], :])
        tokens = mul(gathers[group], jnp.concatenate(pieces, axis=0))
        wide = 128 if group != "B" else 256
        mask = head_cols[:, :128] if group != "B" else head_cols[:, 128:]
        for level in range(2):
            lo = SLOT[name] + level * wide
            level_tokens = jnp.concatenate([tokens[level * 72 : level * 72 + 72], tokens[144:]], axis=1)
            level_tokens = level_tokens.astype(BF16)
            keys = mul(level_tokens, w_keys[level]).astype(BF16)
            values_t = mul_t(w_values_t[level], level_tokens).astype(BF16)
            scores = mul_t(keys, queries[lo : lo + wide, :]) * SCALE + bias[:, lo : lo + wide]
            weights = jnp.exp(scores - jnp.max(scores, axis=0, keepdims=True))
            probs = weights * (1.0 / jnp.sum(weights, axis=0, keepdims=True))
            mixed[:, lo : lo + wide] = (mul(values_t, probs.astype(BF16)) * mask).astype(BF16)

    tables_in[1].wait()
    tab2[...] = jnp.zeros_like(tab2)
    for head in range(12):
        tab2[head : head + 1, :3312] = table_2[head]
    on_left = lon % 2 == 0
    rows2 = by_step(tab2[...], 23)
    copies[3].wait()
    pick2, rep_c, lane_c = const.pick2(), const.rep_c(), const.lane_c().astype(F32)
    for part in range(2):
        steps = rows2[96:272] if part == 0 else jnp.where(on_left, rows2[:176], rows2[192:])
        high, low = split(steps)
        value = merged((picked(pick2, high), picked(pick2, low)), rep_c, lane_c)
        for key_col in range(6):
            first = part * 72 + key_col * 12
            bias2[first : first + 12, :] = shifted(value, (5 - key_col) * 144, 896)[:12]

    w_proj1, w_fc1, w_fc2 = get.w_proj1(), get.w_fc1(), get.w_fc2()
    gain2 = get.ln2_gain()[...]
    merge_gain = get.merge_gain()[...]
    merge_gain = jnp.concatenate([merge_gain[i : i + 1] for i in range(6)], axis=1)
    merge_gain = jnp.broadcast_to(merge_gain, (8, 768))
    w_merge = get.w_merge()
    gain3 = get.ln3_gain()[...]
    gain3 = jnp.concatenate([gain3[i : i + 1] for i in range(3)], axis=1)
    w_qkv2, w_proj2 = get.w_qkv2(), get.w_proj2()
    w_value2_t = mul_t(unit(384), w_qkv2[:, 768:]).astype(BF16)

    sends[0].wait()
    sends[1].wait()
    attend("LB")
    attend("RB")
    collect = const.collect()

    def collected(first, end):
        return mul_t(collect[:, first:end], mixed[:, first:end])

    heads = collected(SLOT["LB"], SLOT["LC"]) + collected(SLOT["RB"], SLOT["RC"])
    table_copy.wait()
    value = merged((table_got[...],), rep_a, lane_a)
    lay_bias("A", jnp.where(jnp.logical_and(key_row < 3, lat == 0), -1e9, value))
    for send in sends[2:]:
        send.wait()
    for name in ("LC", "RC", "LA", "RA"):
        attend(name)

    heads += collected(0, SLOT["LB"]) + collected(SLOT["LC"], SLOT["RB"]) + collected(SLOT["RC"], LANES)
    hidden = own + mul(heads.astype(BF16), w_proj1[...])
    normed2 = norm(hidden, gain2).astype(BF16)
    inner = mul(normed2, w_fc1[...])
    expanded = (0.5 * inner * (1.0 + lax.erf(inner * (0.5**0.5)))).astype(BF16)
    fine_rows = (hidden + mul_t(expanded, w_fc2[...])).astype(BF16)

    fine = fine_rows.astype(F32)
    patches = [fine[p * 72 : p * 72 + 72] for p in range(4)]
    total = sum(jnp.sum(p, axis=-1, keepdims=True) for p in patches)
    centred = [p - total * (1.0 / 768) for p in patches]
    total = sum(jnp.sum(p * p, axis=-1, keepdims=True) for p in centred)
    factor = lax.rsqrt(total * (1.0 / 768) + 1e-05)
    coarse = None
    for p in range(4):
        part_gain = shifted(merge_gain, p * 192, 192)[:1]
        part = (centred[p] * factor * part_gain).astype(BF16)
        term = mul(part, w_merge[p * 192 : p * 192 + 192])
        coarse = term if coarse is None else coarse + term
    coarse = coarse.astype(BF16)
    normed3 = norm(coarse.astype(F32), gain3)
    rows_sent[...] = below(normed3, 80)
    partner = (lat, lon + 1 - 2 * lax.rem(lon, 2))
    swap = pltpu.make_async_remote_copy(
        src_ref=rows_sent, dst_ref=rows_got, send_sem=send_sem.at[9], recv_sem=recv_sem.at[9],
        device_id=partner, device_id_type=MESH,
    )
    swap.start()

    normed3 = normed3.astype(BF16)
    own_queries2 = below(mul(normed3, w_qkv2[:, :384]), 128)
    queries2 = (mul(const.spread2(), own_queries2) * const.head_rows2().astype(F32)).astype(BF16)
    coarse_pad = mul(const.pad2(), below(coarse.astype(F32), 128))
    head_cols2, collect2 = const.head_cols2().astype(F32), const.collect2()

    def scored(tokens, part):
        keys = mul(tokens, w_qkv2[:, 384:768]).astype(BF16)
        return mul_t(keys, queries2) * SCALE + bias2[part * 72 : part * 72 + 72, :]

    scores_near = scored(normed3, 0)
    values_near = mul_t(w_value2_t, normed3).astype(BF16)
    placed_rows = mul(const.unperm(), fine_rows)
    for token in range(144):
        fine_ref[token] = placed_rows[token * 2 : token * 2 + 2].astype(BF16)
    swap.wait()
    other = rows_got[...].astype(F32)[:72].astype(BF16)
    scores_far = scored(other, 1)
    values_far = mul_t(w_value2_t, other).astype(BF16)
    top = jnp.maximum(
        jnp.max(scores_near, axis=0, keepdims=True), jnp.max(scores_far, axis=0, keepdims=True)
    )
    near = jnp.exp(scores_near - top)
    far = jnp.exp(scores_far - top)
    factor = 1.0 / (jnp.sum(near, axis=0, keepdims=True) + jnp.sum(far, axis=0, keepdims=True))
    blended = mul(values_near, (near * factor).astype(BF16)) + mul(values_far, (far * factor).astype(BF16))
    heads2 = mul_t(collect2, (blended * head_cols2).astype(BF16)).astype(BF16)
    result = coarse_pad + mul(heads2, w_proj2[...])
    for token in range(36):
        coarse_ref[token] = result[token * 2 : token * 2 + 2].astype(BF16)


def shards(
    fine_tokens, ln1_gain, w_qkv1, bias1, w_proj1, ln2_gain, w_fc1, w_fc2, merge_gain, w_merge,
    ln3_gain, w_qkv2, bias2, w_proj2,
):
    ops = dict(
        fine_tokens=fine_tokens.transpose(1, 2, 0, 3).reshape(144, 2, 192),
        ln1_gain=ln1_gain.reshape(1, 192), w_qkv1=w_qkv1, bias1=bias1.reshape(12, 1, 3312),
        w_proj1=w_proj1, ln2_gain=ln2_gain.reshape(1, 192), w_fc1=w_fc1, w_fc2=w_fc2.T,
        merge_gain=merge_gain.reshape(6, 128), w_merge=w_merge, ln3_gain=ln3_gain.reshape(3, 128),
        w_qkv2=w_qkv2, bias2=bias2.reshape(12, 1, 3312), w_proj2=w_proj2,
        pack=jnp.asarray(packed()[0]),
    )
    names = tuple(ops)
    any_space = pl.BlockSpec(memory_space=pl.ANY)
    scratch = [pltpu.VMEM(ops[name].shape, ops[name].dtype) for name in KEPT]
    scratch += [
        pltpu.VMEM(packed()[0].shape, BF16),
        pltpu.VMEM((8, 3328), F32),
        pltpu.VMEM((16, 3328), F32),
        pltpu.VMEM((288, 192), F32),
        pltpu.VMEM((SEG_ROWS, 128), BF16),
        pltpu.VMEM((HALO_ROWS, 128), BF16),
        pltpu.VMEM((48, 184), BF16),
        pltpu.VMEM((48, 184), BF16),
        pltpu.VMEM((12, 1, 3312), F32),
        pltpu.VMEM((12, 1, 3312), F32),
        pltpu.VMEM((LANES, 192), BF16),
        pltpu.VMEM((72, LANES), F32),
        pltpu.VMEM((144, 896), F32),
        pltpu.VMEM((192, LANES), BF16),
        pltpu.VMEM((80, 384), BF16),
        pltpu.VMEM((80, 384), BF16),
        pltpu.SemaphoreType.DMA((len(LOADED),)),
        pltpu.SemaphoreType.DMA((2,)),
        pltpu.SemaphoreType.DMA((10,)),
        pltpu.SemaphoreType.DMA((10,)),
    ]
    fine, coarse = pl.pallas_call(
        functools.partial(kernel, names),
        out_shape=(
            pltpu.VMEM((144, 2, 192), BF16),
            pltpu.VMEM((36, 2, 384), BF16),
        ),
        in_specs=[pl.BlockSpec(memory_space=pl.ANY)] * len(names),
        out_specs=(pl.BlockSpec(memory_space=pltpu.VMEM),) * 2,
        scratch_shapes=scratch,
        compiler_params=pltpu.CompilerParams(
            collective_id=0, has_side_effects=True, vmem_limit_bytes=56 * 1024 * 1024
        ),
        cost_estimate=pl.CostEstimate(
            flops=2_000_000_000, bytes_accessed=12_000_000, transcendentals=1_000_000
        ),
    )(*ops.values())
    fine = fine.reshape(12, 12, 2, 192).transpose(2, 0, 1, 3)
    return fine, coarse.reshape(6, 6, 2, 384).transpose(2, 0, 1, 3)


def solution(mesh):
    whole, by_lat, grid = P(), P("lat", None, None, None), P(None, "lat", "lon", None)
    in_specs = (grid, whole, whole, by_lat) + (whole,) * 8 + (by_lat, whole)
    return jax.shard_map(
        shards, mesh=mesh, in_specs=in_specs, out_specs=(grid, grid), check_vma=False
    )
```
